256 devices in a mesh: island: 8 (over y_lo, x), fsdp: 32 (over z, y_hi, core).
Axes of the slice: x: 4, y: 4 (y_hi: 2, y_lo: 2; y = y_hi * 2 + y_lo), z: 8, core: 2. Of those that a mesh axis runs over, the one named last changes fastest.
Arguments:
- tokens: bfloat16 [65536, 4096], P(('island', 'fsdp')), may hold values from -6 to 6
- target: bfloat16 [65536, 1024], P(('island', 'fsdp')), may hold values from -6 to 6
- kv_weight: bfloat16 [8, 4096, 1024], P('island', 'fsdp'), may hold values from -0.09375 to 0.09375
- norm_gain: float32 [8, 4096], P('island'), may hold values from 0.5 to 1.5
- global_frag: float32 [2, 4096, 1024], P(None, 'fsdp'), may hold values from -6 to 6
- momentum: float32 [2, 4096, 1024], P(None, 'fsdp'), may hold values from -3 to 3
- local_frag: float32 [8, 2, 4096, 1024], P('island', None, 'fsdp'), may hold values from -6 to 6
Outputs:
- weight_grad: bfloat16 [8, 4096, 1024], P('island', 'fsdp')
- token_grad: bfloat16 [65536, 4096], P(('island', 'fsdp'))
- gain_grad: float32 [8, 4096], P('island')
- new_global: float32 [2, 4096, 1024], P(None, 'fsdp')
- new_momentum: float32 [2, 4096, 1024], P(None, 'fsdp')
The draws below stay inside these ranges and needn't reach their ends.
All inputs are finite; a program needn't handle non-finite values.
Results may differ from the reference program's by a relative error of at most 0.0055.
Values may be sent and summed in bfloat16 or wider, within the bound.
A program may use at most 128 MiB of HBM per device.

```python
import jax
import jax.numpy as jnp
from jax import lax

D = 4096
FRAG = 2
KVW = 1024
ISLANDS = 8
ISL_TOKENS = 8192
TOKENS = 65536


def block_levels(rng, shape, split, smallest, top_value):
    def one(position, shards_of):
        draws = jax.random.uniform(jax.random.fold_in(jax.random.fold_in(rng, 6), position), (shards_of,), jnp.float32, smallest / len(split), top_value / len(split))
        return jnp.repeat(jnp.exp(draws), shape[position] // shards_of).reshape((-1,) + (1,) * (len(shape) - position - 1))

    level = one(*split[0])
    for cut in split[1:]:
        level = level * one(*cut)
    return level


def centred(rng, shape, scale, bound, pieces=(), kind=jnp.bfloat16):
    array = scale * jax.random.normal(rng, shape, jnp.float32)
    if pieces:
        array = array * block_levels(rng, shape, pieces, -0.22, 0.18)
    return jnp.clip(array, -bound, bound).astype(kind)


def setup_inputs(seed: int = 0) -> dict:
    splits = jax.random.split(jax.random.key(seed), 8)
    return {
        "tokens": centred(splits[0], (TOKENS, D), 1.0, 6.0, ((0, 256),)),
        "target": centred(splits[1], (TOKENS, KVW), 1.0, 6.0, ((0, 256),)),
        "kv_weight": centred(splits[2], (ISLANDS, D, KVW), D ** -0.5, 0.09375, ((0, 8), (1, 32))),
        "norm_gain": jnp.clip(1.0 + 0.1 * jax.random.normal(splits[3], (ISLANDS, D), jnp.float32), 0.5, 1.5),
        "global_frag": centred(splits[4], (FRAG, D, KVW), 1.0, 6.0, ((1, 32),), jnp.float32),
        "momentum": centred(splits[5], (FRAG, D, KVW), 0.5, 3.0, ((1, 32),), jnp.float32),
        "local_frag": centred(splits[6], (ISLANDS, FRAG, D, KVW), 1.0, 6.0, ((0, 8), (2, 32)), jnp.float32),
    }


def one_replica(packed):
    tokens, target, weight, gain = packed
    tokens_f = tokens.astype(jnp.float32)
    inverse = lax.rsqrt(lax.optimization_barrier(jnp.mean(tokens_f * tokens_f, axis=1, keepdims=True)) + 1e-05)
    scaled = tokens_f * inverse
    normed = (scaled * gain[None, :]).astype(jnp.bfloat16)
    projected = jnp.dot(normed, weight, preferred_element_type=jnp.float32)
    error = (projected - target.astype(jnp.float32)).astype(jnp.bfloat16)
    loss_scale = 1.0 / jnp.sqrt(jnp.float32(ISL_TOKENS))
    product = lax.dot_general(normed, error, (((0,), (0,)), ((), ())), preferred_element_type=jnp.float32)
    grad_weight = (loss_scale * product).astype(jnp.bfloat16)
    back = lax.dot_general(error, weight, (((1,), (1,)), ((), ())), preferred_element_type=jnp.float32)
    grad_gain = lax.optimization_barrier(jnp.sum(back * scaled, axis=0))
    weighted = back * gain[None, :]
    token_grad = inverse * (weighted - scaled * lax.optimization_barrier(jnp.mean(weighted * scaled, axis=1, keepdims=True)))
    return (grad_weight, token_grad.astype(jnp.bfloat16), grad_gain)

def reference(tokens, target, kv_weight, norm_gain, global_frag, momentum, local_frag):
    stacked = (tokens.reshape(ISLANDS, ISL_TOKENS, D), target.reshape(ISLANDS, ISL_TOKENS, KVW), kv_weight, norm_gain)
    weight_grad, token_grad, gain_grad = lax.map(one_replica, stacked)
    token_grad = token_grad.reshape(TOKENS, D)
    outer_grad = lax.optimization_barrier(jnp.sum(global_frag[None] - local_frag, axis=0)) / ISLANDS
    new_momentum = 0.9 * momentum + outer_grad
    new_global = global_frag - 0.7 * (outer_grad + 0.9 * new_momentum)
    return (weight_grad, token_grad, gain_grad, new_global, new_momentum)
```

```python
import math

import jax
import jax.numpy as jnp
from jax import lax
from jax.experimental import pallas as pl
from jax.experimental.pallas import tpu as pltpu
from jax.sharding import PartitionSpec as P

MESH = pl.DeviceIdType.MESH
BF16 = jnp.bfloat16
F32 = jnp.float32
NQ = 4
QC = 256
NZ = 8
TOK = 256
D = 4096
PLUS, MINUS = 0, 1
NSEND = 160


def hops(q, way):
    return 4 if (q % 2) == way else 3


def nt_dot(a, b):
    return lax.dot_general(a, b, (((1,), (1,)), ((), ())), preferred_element_type=F32)


def kernel(
    tok_h, tgt_h, w_h, gain_h, glob_h, mom_h, loc_h,
    wg_h, tg_h, gg_h, ng_h, nm_h,
    tok, tgt, gain, glob, mom, loc, wb, normed, nto, ntr, errb, rss, rsr, back, tgo, wgo,
    ds, dr, osb, go, gc, g1, gy, g2, gz, gsum, rowacc, inv_ref,
    ld, st, send, ag_sem, y_sem, sib_sem, nt_sem, err_sem, rs_sem, d_sem, o_sem, g_sem, gz_sem,
):
    isl = lax.axis_index("island")
    fs = lax.axis_index("fsdp")
    z = fs // 4
    yh = (fs // 2) % 2
    c = fs % 2

    def at(zz, yy, cc):
        return (isl, (zz * 2 + yy) * 2 + cc)

    def mod8(v):
        return lax.rem(v + 8, 8)

    ring = (at(mod8(z + 1), yh, c), at(mod8(z - 1), yh, c))
    sib = at(z, yh, 1 - c)
    flip = at(z, 1 - yh, c)
    diag = at(z, 1 - yh, 1 - c)

    sends = []

    def push(src, dst, sem, dev):
        cp = pltpu.make_async_remote_copy(
            src_ref=src, dst_ref=dst, send_sem=send.at[len(sends)], recv_sem=sem,
            device_id=dev, device_id_type=MESH)
        cp.start()
        sends.append(cp)

    def arrived(ref, sem):
        pltpu.make_async_copy(ref, ref, sem).wait()

    loads_w = [pltpu.make_async_copy(
        w_h.at[:, pl.ds(q * QC, QC)], wb.at[q, c, z, pl.ds(yh * 128, 128)], ld.at[q]) for q in range(NQ)]
    for cp in loads_w:
        cp.start()
    loads = [pltpu.make_async_copy(s, d, ld.at[NQ + i]) for i, (s, d) in enumerate(
        ((tok_h, tok), (gain_h, gain), (tgt_h, tgt), (glob_h, glob), (loc_h, loc), (mom_h, mom)))]
    for cp in loads:
        cp.start()

    bar = pltpu.get_barrier_semaphore()
    partners = [at(mod8(z + o), yh, c) for o in range(1, NZ)] + [sib, flip, diag]
    partners += [(lax.rem(isl + o, 8), fs) for o in range(1, 8)]
    for dev in partners:
        pl.semaphore_signal(bar, inc=1, device_id=dev, device_id_type=MESH)
    pl.semaphore_wait(bar, len(partners))

    def own_half(q, yy):
        return wb.at[q, c, z, pl.ds(yy * 128, 128)]

    def ring_own(q, yy):
        for way in (PLUS, MINUS):
            push(own_half(q, yy), own_half(q, yy), ag_sem.at[q, way, 0], ring[way])

    for q in range(NQ):
        loads_w[q].wait()
        push(own_half(q, yh), own_half(q, yh), y_sem.at[q], flip)
        if q < 2:
            ring_own(q, yh)

    def to_sib(q, zz):
        push(wb.at[q, c, zz], wb.at[q, c, zz], sib_sem.at[q], sib)

    def ring_other(q):
        arrived(own_half(q, 1 - yh), y_sem.at[q])
        ring_own(q, 1 - yh)

    loads[0].wait()

    def squares(i, acc):
        t = tok[:, pl.ds(pl.multiple_of(i * 128, 128), 128)].astype(F32)
        return acc + t * t

    acc = lax.fori_loop(0, 32, squares, jnp.zeros((TOK, 128), F32), unroll=4)
    inv_ref[...] = jnp.broadcast_to(
        lax.rsqrt(jnp.sum(acc, axis=1, keepdims=True) / D + 1e-05), (TOK, 128))

    for q in (0, 1):
        ring_other(q)
    for q in (0, 1):
        to_sib(q, z)

    loads[1].wait()

    def norm_block(i, _):
        bc, bz, by = i // 16, (i // 2) % 8, i % 2
        f = (bz * 2 + by) * 2 + bc
        cols = pl.ds(pl.multiple_of(f * 128, 128), 128)
        n = (tok[:, cols].astype(F32) * inv_ref[...] * gain[:, cols]).astype(BF16)
        normed[:, pl.ds(pl.multiple_of(i * 128, 128), 128)] = n
        nto[by, bc, bz] = n.T
        return 0

    lax.fori_loop(0, 32, norm_block, 0, unroll=2)
    push(nto.at[yh, 1 - c], ntr.at[0], nt_sem.at[0], sib)
    push(nto.at[1 - yh, c], ntr.at[1], nt_sem.at[1], flip)
    push(nto.at[1 - yh, 1 - c], ntr.at[2], nt_sem.at[2], diag)

    def gather_step(half, s):
        for q in (2 * half, 2 * half + 1):
            for way in (PLUS, MINUS):
                k = hops(q, way)
                if s > k:
                    continue
                zz = mod8(z - s) if way == PLUS else mod8(z + s)
                arrived(wb.at[q, c, zz], ag_sem.at[q, way, s - 1])
                if s < k:
                    push(wb.at[q, c, zz], wb.at[q, c, zz], ag_sem.at[q, way, s], ring[way])
                to_sib(q, zz)

    def project(half):
        for q in (2 * half, 2 * half + 1):
            arrived(wb.at[q, 1 - c], sib_sem.at[q])
            p = jnp.dot(normed[...], wb[q].reshape(D, QC), preferred_element_type=F32)
            errb[0, q] = (p - tgt[:, q * QC:(q + 1) * QC].astype(F32)).astype(BF16)
            push(errb.at[0, q], errb.at[2, q], err_sem.at[1, q], flip)
            push(errb.at[0, q], errb.at[1, q], err_sem.at[0, q], sib)

    def pass_error(half):
        for q in (2 * half, 2 * half + 1):
            arrived(errb.at[2, q], err_sem.at[1, q])
            push(errb.at[2, q], errb.at[3, q], err_sem.at[2, q], sib)

    def have_error(half):
        for q in (2 * half, 2 * half + 1):
            arrived(errb.at[1, q], err_sem.at[0, q])
            arrived(errb.at[3, q], err_sem.at[2, q])

    def term(q, zz):
        p = jnp.dot(nto[yh, c, zz], errb[0, q], preferred_element_type=F32)
        for r in range(3):
            p += jnp.dot(ntr[r, zz], errb[r + 1, q], preferred_element_type=F32)
        return p

    def reduce_step(half, s):
        for q in (2 * half, 2 * half + 1):
            for way in (PLUS, MINUS):
                k = hops(q, way)
                if s >= k:
                    continue
                p = term(q, mod8(z + (k - s)) if way == PLUS else mod8(z - (k - s)))
                if s > 0:
                    arrived(rsr.at[q, way, s - 1], rs_sem.at[q, way, s - 1])
                    p += rsr[q, way, s - 1].astype(F32)
                rss[q, way, s] = p.astype(BF16)
                push(rss.at[q, way, s], rsr.at[q, way, s], rs_sem.at[q, way, s], ring[way])

    loss_scale = 1.0 / math.sqrt(TOK * 32)

    def reduce_last(half):
        for q in (2 * half, 2 * half + 1):
            p = term(q, z)
            for way in (PLUS, MINUS):
                s = hops(q, way) - 1
                arrived(rsr.at[q, way, s], rs_sem.at[q, way, s])
                p += rsr[q, way, s].astype(F32)
            wgo[:, q * QC:(q + 1) * QC] = (p * loss_scale).astype(BF16)

    def drift_out():
        loads[3].wait()
        loads[4].wait()

        def one(j, _):
            rows = pl.ds(pl.multiple_of(j * 32, 32), 32)
            ds[j] = (glob[rows, :] - loc[rows, :]).astype(BF16)
            return 0

        lax.fori_loop(0, 8, one, 0)
        for o in range(1, 8):
            j = lax.rem(isl + o, 8)
            push(ds.at[j], dr.at[isl], d_sem.at[isl], (j, fs))
        dr[isl] = ds[isl]

    def drift_sum():
        for o in range(1, 8):
            j = lax.rem(isl + o, 8)
            arrived(dr.at[j], d_sem.at[j])
        total = dr[0].astype(F32)
        for j in range(1, 8):
            total += dr[j].astype(F32)
        osb[isl] = (total / 8).astype(BF16)
        for o in range(1, 8):
            j = lax.rem(isl + o, 8)
            push(osb.at[isl], osb.at[isl], o_sem.at[isl], (j, fs))

    def outer_step():
        loads[5].wait()
        for o in range(1, 8):
            j = lax.rem(isl + o, 8)
            arrived(osb.at[j], o_sem.at[j])

        def one(j, _):
            rows = pl.ds(pl.multiple_of(j * 32, 32), 32)
            outer = osb[j].astype(F32)
            nm = 0.9 * mom[rows, :] + outer
            mom[rows, :] = nm
            glob[rows, :] = glob[rows, :] - 0.7 * (outer + 0.9 * nm)
            return 0

        lax.fori_loop(0, 8, one, 0)
        stores.append(pltpu.make_async_copy(mom, nm_h, st.at[0]))
        stores[-1].start()
        stores.append(pltpu.make_async_copy(glob, ng_h, st.at[1]))
        stores[-1].start()

    stores = []

    def back_blocks(lo, hi):
        def one(kb, _):
            bc, bz = kb // 8, kb % 8
            b = nt_dot(errb[0, 0], wb[0, bc, bz])
            for q in range(1, NQ):
                b += nt_dot(errb[0, q], wb[q, bc, bz])
            for by in range(2):
                f = (bz * 2 + by) * 2 + bc
                cols = pl.ds(pl.multiple_of(f * 128, 128), 128)
                bb = b[:, by * 128:(by + 1) * 128]
                sc = tok[:, cols].astype(F32) * inv_ref[...]
                bs = bb * sc
                go[pl.ds(f, 1), :] = jnp.sum(bs, axis=0, keepdims=True)
                rowacc[...] += bs * gain[:, cols]
                back[:, cols] = bb
            return 0

        lax.fori_loop(lo, hi, one, 0)

    def token_grad():
        m = jnp.sum(rowacc[...], axis=1, keepdims=True) / D

        def one(f, _):
            cols = pl.ds(pl.multiple_of(f * 128, 128), 128)
            iv = inv_ref[...]
            sc = tok[:, cols].astype(F32) * iv
            tgo[:, cols] = (iv * (back[:, cols] * gain[:, cols] - sc * m)).astype(BF16)
            return 0

        lax.fori_loop(0, 32, one, 0)
        stores.append(pltpu.make_async_copy(tgo, tg_h, st.at[2]))
        stores[-1].start()

    gather_step(0, 1)
    drift_out()
    gather_step(0, 2)
    for q in (2, 3):
        ring_own(q, yh)
        ring_other(q)
    for q in (2, 3):
        to_sib(q, z)
    gather_step(0, 3)
    loads[2].wait()
    gather_step(0, 4)
    project(0)
    gather_step(1, 1)
    pass_error(0)
    drift_sum()
    gather_step(1, 2)
    have_error(0)
    for r in range(3):
        arrived(ntr.at[r], nt_sem.at[r])
    gather_step(1, 3)
    outer_step()
    gather_step(1, 4)
    reduce_step(0, 0)
    project(1)
    reduce_step(0, 1)
    pass_error(1)
    rowacc[...] = jnp.zeros_like(rowacc)
    reduce_step(0, 2)
    have_error(1)
    reduce_step(1, 0)
    back_blocks(0, 8)
    reduce_step(0, 3)
    reduce_step(1, 1)
    back_blocks(8, 16)
    push(go, gc, g_sem.at[0], sib)
    reduce_step(1, 2)
    arrived(gc, g_sem.at[0])
    g1[...] = go[...] + gc[...]
    push(g1, gy, g_sem.at[1], flip)
    reduce_last(0)
    reduce_step(1, 3)
    arrived(gy, g_sem.at[1])
    g2[...] = g1[...] + gy[...]
    for o in range(1, NZ):
        push(g2, gz.at[z], gz_sem.at[z], at(mod8(z + o), yh, c))
    gz[z] = g2[...]
    token_grad()
    reduce_last(1)
    stores.append(pltpu.make_async_copy(wgo, wg_h, st.at[3]))
    stores[-1].start()
    for o in range(1, NZ):
        zz = mod8(z + o)
        arrived(gz.at[zz], gz_sem.at[zz])
    total = gz[0]
    for j in range(1, NZ):
        total += gz[j]
    gsum[...] = total
    stores.append(pltpu.make_async_copy(gsum, gg_h, st.at[4]))
    stores[-1].start()
    for cp in sends:
        cp.wait_send()
    for cp in stores:
        cp.wait()


def on_device(tokens, target, kv_weight, norm_gain, global_frag, momentum, local_frag):
    sem = pltpu.SemaphoreType.DMA
    vm = pltpu.VMEM
    anyspec = pl.BlockSpec(memory_space=pl.ANY)
    outs = (
        jax.ShapeDtypeStruct((128, 1024), BF16),
        jax.ShapeDtypeStruct((TOK, D), BF16),
        jax.ShapeDtypeStruct((32, 128), F32),
        jax.ShapeDtypeStruct((256, 1024), F32),
        jax.ShapeDtypeStruct((256, 1024), F32),
    )
    wg, tg, gg, ng, nm = pl.pallas_call(
        kernel,
        out_shape=outs,
        in_specs=[anyspec] * 7,
        out_specs=[anyspec] * 5,
        scratch_shapes=[
            vm((TOK, D), BF16),
            vm((TOK, 1024), BF16),
            vm((1, D), F32),
            vm((256, 1024), F32),
            vm((256, 1024), F32),
            vm((256, 1024), F32),
            vm((NQ, 2, NZ, 256, QC), BF16),
            vm((TOK, D), BF16),
            vm((2, 2, NZ, 128, TOK), BF16),
            vm((3, NZ, 128, TOK), BF16),
            vm((4, NQ, TOK, QC), BF16),
            vm((NQ, 2, 4, 128, QC), BF16),
            vm((NQ, 2, 4, 128, QC), BF16),
            vm((TOK, D), F32),
            vm((TOK, D), BF16),
            vm((128, 1024), BF16),
            vm((8, 32, 1024), BF16),
            vm((8, 32, 1024), BF16),
            vm((8, 32, 1024), BF16),
            vm((32, 128), F32),
            vm((32, 128), F32),
            vm((32, 128), F32),
            vm((32, 128), F32),
            vm((32, 128), F32),
            vm((NZ, 32, 128), F32),
            vm((32, 128), F32),
            vm((TOK, 128), F32),
            vm((TOK, 128), F32),
            sem((NQ + 6,)),
            sem((5,)),
            sem((NSEND,)),
            sem((NQ, 2, 4)),
            sem((NQ,)),
            sem((NQ,)),
            sem((3,)),
            sem((3, NQ)),
            sem((NQ, 2, 4)),
            sem((8,)),
            sem((8,)),
            sem((2,)),
            sem((NZ,)),
        ],
        compiler_params=pltpu.CompilerParams(
            collective_id=0, has_side_effects=True, vmem_limit_bytes=60 * 2**20),
        cost_estimate=pl.CostEstimate(flops=6 * 2**30, bytes_accessed=12 * 2**20, transcendentals=256),
        name="step",
    )(
        tokens, target, kv_weight[0], norm_gain,
        global_frag.reshape(256, 1024), momentum.reshape(256, 1024), local_frag.reshape(256, 1024),
    )
    return (wg[None], tg, gg.reshape(1, D), ng.reshape(2, 128, 1024), nm.reshape(2, 128, 1024))


def solution(mesh):
    placed = (
        P(("island", "fsdp"), None),
        P(("island", "fsdp"), None),
        P("island", "fsdp", None),
        P("island", None),
        P(None, "fsdp", None),
        P(None, "fsdp", None),
        P("island", None, "fsdp", None),
    )
    return jax.shard_map(
        on_device,
        mesh=mesh,
        in_specs=placed,
        out_specs=(
            P("island", "fsdp", None),
            P(("island", "fsdp"), None),
            P("island", None),
            P(None, "fsdp", None),
            P(None, "fsdp", None),
        ),
        check_vma=False,
    )
```

```python
import math

import jax
import jax.numpy as jnp
from jax import lax
from jax.experimental import pallas as pl
from jax.experimental.pallas import tpu as pltpu
from jax.sharding import PartitionSpec as P

MESH = pl.DeviceIdType.MESH
BF16 = jnp.bfloat16
F32 = jnp.float32
NQ = 4
QC = 256
NZ = 8
TOK = 256
D = 4096
PLUS, MINUS = 0, 1
NSEND = 160


def hops(q, way):
    return 4 if (q % 2) == way else 3


def nt_dot(a, b):
    return lax.dot_general(a, b, (((1,), (1,)), ((), ())), preferred_element_type=F32)


def kernel(
    tok_h, tgt_h, w_h, gain_h, glob_h, mom_h, loc_h,
    wg_h, tg_h, gg_h, ng_h, nm_h,
    tok, tgt, gain, glob, mom, loc, wb, normed, nto, ntr, errb, rss, rsr, back, tgo, wgo,
    ds, dr, osb, go, gc, g1, gy, g2, gz, gsum, rowacc, inv_ref,
    ld, st, send, ag_sem, y_sem, sib_sem, nt_sem, err_sem, rs_sem, d_sem, o_sem, g_sem, gz_sem,
):
    isl = lax.axis_index("island")
    fs = lax.axis_index("fsdp")
    z = fs // 4
    yh = (fs // 2) % 2
    c = fs % 2

    def at(zz, yy, cc):
        return (isl, (zz * 2 + yy) * 2 + cc)

    def mod8(v):
        return lax.rem(v + 8, 8)

    ring = (at(mod8(z + 1), yh, c), at(mod8(z - 1), yh, c))
    sib = at(z, yh, 1 - c)
    flip = at(z, 1 - yh, c)
    diag = at(z, 1 - yh, 1 - c)

    sends = []

    def push(src, dst, sem, dev):
        cp = pltpu.make_async_remote_copy(
            src_ref=src, dst_ref=dst, send_sem=send.at[len(sends)], recv_sem=sem,
            device_id=dev, device_id_type=MESH)
        cp.start()
        sends.append(cp)

    def arrived(ref, sem):
        pltpu.make_async_copy(ref, ref, sem).wait()

    loads_w = [pltpu.make_async_copy(
        w_h.at[:, pl.ds(q * QC, QC)], wb.at[q, c, z, pl.ds(yh * 128, 128)], ld.at[q]) for q in range(NQ)]
    for cp in loads_w:
        cp.start()
    loads = [pltpu.make_async_copy(s, d, ld.at[NQ + i]) for i, (s, d) in enumerate(
        ((tok_h, tok), (gain_h, gain), (tgt_h, tgt), (glob_h, glob), (loc_h, loc), (mom_h, mom)))]
    for cp in loads:
        cp.start()

    bar = pltpu.get_barrier_semaphore()
    partners = [at(mod8(z + o), yh, c) for o in range(1, NZ)] + [sib, flip, diag]
    partners += [(lax.rem(isl + o, 8), fs) for o in range(1, 8)]
    for dev in partners:
        pl.semaphore_signal(bar, inc=1, device_id=dev, device_id_type=MESH)
    pl.semaphore_wait(bar, len(partners))

    def own_half(q, yy):
        return wb.at[q, c, z, pl.ds(yy * 128, 128)]

    def ring_own(q, yy):
        for way in (PLUS, MINUS):
            push(own_half(q, yy), own_half(q, yy), ag_sem.at[q, way, 0], ring[way])

    for q in range(NQ):
        loads_w[q].wait()
        push(own_half(q, yh), own_half(q, yh), y_sem.at[q], flip)
        if q < 3:
            ring_own(q, yh)

    def to_sib(q, zz):
        push(wb.at[q, c, zz], wb.at[q, c, zz], sib_sem.at[q], sib)

    def ring_other(q):
        arrived(own_half(q, 1 - yh), y_sem.at[q])
        ring_own(q, 1 - yh)

    loads[0].wait()

    def squares(i, acc):
        t = tok[:, pl.ds(pl.multiple_of(i * 128, 128), 128)].astype(F32)
        return acc + t * t

    acc = lax.fori_loop(0, 32, squares, jnp.zeros((TOK, 128), F32), unroll=4)
    inv_ref[...] = jnp.broadcast_to(
        lax.rsqrt(jnp.sum(acc, axis=1, keepdims=True) / D + 1e-05), (TOK, 128))

    for q in (0, 1):
        ring_other(q)
    for q in (0, 1):
        to_sib(q, z)

    loads[1].wait()

    def norm_block(i, _):
        bc, bz, by = i // 16, (i // 2) % 8, i % 2
        f = (bz * 2 + by) * 2 + bc
        cols = pl.ds(pl.multiple_of(f * 128, 128), 128)
        n = (tok[:, cols].astype(F32) * inv_ref[...] * gain[:, cols]).astype(BF16)
        normed[:, pl.ds(pl.multiple_of(i * 128, 128), 128)] = n
        nto[by, bc, bz] = n.T
        return 0

    lax.fori_loop(0, 32, norm_block, 0, unroll=2)
    push(nto.at[yh, 1 - c], ntr.at[0], nt_sem.at[0], sib)
    push(nto.at[1 - yh, c], ntr.at[1], nt_sem.at[1], flip)
    push(nto.at[1 - yh, 1 - c], ntr.at[2], nt_sem.at[2], diag)

    def gather_step(half, s):
        for q in (2 * half, 2 * half + 1):
            for way in (PLUS, MINUS):
                k = hops(q, way)
                if s > k:
                    continue
                zz = mod8(z - s) if way == PLUS else mod8(z + s)
                arrived(wb.at[q, c, zz], ag_sem.at[q, way, s - 1])
                if s < k:
                    push(wb.at[q, c, zz], wb.at[q, c, zz], ag_sem.at[q, way, s], ring[way])
                to_sib(q, zz)

    def project(half):
        for q in (2 * half, 2 * half + 1):
            arrived(wb.at[q, 1 - c], sib_sem.at[q])
            p = jnp.dot(normed[...], wb[q].reshape(D, QC), preferred_element_type=F32)
            errb[0, q] = (p - tgt[:, q * QC:(q + 1) * QC].astype(F32)).astype(BF16)
            push(errb.at[0, q], errb.at[2, q], err_sem.at[1, q], flip)
            push(errb.at[0, q], errb.at[1, q], err_sem.at[0, q], sib)

    def pass_error(half):
        for q in (2 * half, 2 * half + 1):
            arrived(errb.at[2, q], err_sem.at[1, q])
            push(errb.at[2, q], errb.at[3, q], err_sem.at[2, q], sib)

    def have_error(half):
        for q in (2 * half, 2 * half + 1):
            arrived(errb.at[1, q], err_sem.at[0, q])
            arrived(errb.at[3, q], err_sem.at[2, q])

    def term(q, zz):
        p = jnp.dot(nto[yh, c, zz], errb[0, q], preferred_element_type=F32)
        for r in range(3):
            p += jnp.dot(ntr[r, zz], errb[r + 1, q], preferred_element_type=F32)
        return p

    def reduce_step(half, s):
        for q in (2 * half, 2 * half + 1):
            for way in (PLUS, MINUS):
                k = hops(q, way)
                if s >= k:
                    continue
                p = term(q, mod8(z + (k - s)) if way == PLUS else mod8(z - (k - s)))
                if s > 0:
                    arrived(rsr.at[q, way, s - 1], rs_sem.at[q, way, s - 1])
                    p += rsr[q, way, s - 1].astype(F32)
                rss[q, way, s] = p.astype(BF16)
                push(rss.at[q, way, s], rsr.at[q, way, s], rs_sem.at[q, way, s], ring[way])

    loss_scale = 1.0 / math.sqrt(TOK * 32)

    def reduce_last(half):
        for q in (2 * half, 2 * half + 1):
            p = term(q, z)
            for way in (PLUS, MINUS):
                s = hops(q, way) - 1
                arrived(rsr.at[q, way, s], rs_sem.at[q, way, s])
                p += rsr[q, way, s].astype(F32)
            wgo[:, q * QC:(q + 1) * QC] = (p * loss_scale).astype(BF16)

    def drift_out():
        loads[3].wait()
        loads[4].wait()

        def one(j, _):
            rows = pl.ds(pl.multiple_of(j * 32, 32), 32)
            ds[j] = (glob[rows, :] - loc[rows, :]).astype(BF16)
            return 0

        lax.fori_loop(0, 8, one, 0)
        for o in range(1, 8):
            j = lax.rem(isl + o, 8)
            push(ds.at[j], dr.at[isl], d_sem.at[isl], (j, fs))
        dr[isl] = ds[isl]

    def drift_sum():
        for o in range(1, 8):
            j = lax.rem(isl + o, 8)
            arrived(dr.at[j], d_sem.at[j])
        total = dr[0].astype(F32)
        for j in range(1, 8):
            total += dr[j].astype(F32)
        osb[isl] = (total / 8).astype(BF16)
        for o in range(1, 8):
            j = lax.rem(isl + o, 8)
            push(osb.at[isl], osb.at[isl], o_sem.at[isl], (j, fs))

    def outer_step():
        loads[5].wait()
        for o in range(1, 8):
            j = lax.rem(isl + o, 8)
            arrived(osb.at[j], o_sem.at[j])

        def one(j, _):
            rows = pl.ds(pl.multiple_of(j * 32, 32), 32)
            outer = osb[j].astype(F32)
            nm = 0.9 * mom[rows, :] + outer
            mom[rows, :] = nm
            glob[rows, :] = glob[rows, :] - 0.7 * (outer + 0.9 * nm)
            return 0

        lax.fori_loop(0, 8, one, 0)
        stores.append(pltpu.make_async_copy(mom, nm_h, st.at[0]))
        stores[-1].start()
        stores.append(pltpu.make_async_copy(glob, ng_h, st.at[1]))
        stores[-1].start()

    stores = []

    def back_first(lo, hi):
        def one(kb, _):
            bc, bz = kb // 8, kb % 8
            b = nt_dot(errb[0, 0], wb[0, bc, bz]) + nt_dot(errb[0, 1], wb[1, bc, bz])
            back[:, pl.ds(pl.multiple_of(kb * 256, 256), 256)] = b
            return 0

        lax.fori_loop(lo, hi, one, 0)

    def back_rest(lo, hi):
        def one(kb, _):
            bc, bz = kb // 8, kb % 8
            here = pl.ds(pl.multiple_of(kb * 256, 256), 256)
            b = back[:, here] + nt_dot(errb[0, 2], wb[2, bc, bz]) + nt_dot(errb[0, 3], wb[3, bc, bz])
            back[:, here] = b
            for by in range(2):
                f = (bz * 2 + by) * 2 + bc
                cols = pl.ds(pl.multiple_of(f * 128, 128), 128)
                bs = b[:, by * 128:(by + 1) * 128] * (tok[:, cols].astype(F32) * inv_ref[...])
                go[pl.ds(f, 1), :] = jnp.sum(bs, axis=0, keepdims=True)
                rowacc[...] += bs * gain[:, cols]
            return 0

        lax.fori_loop(lo, hi, one, 0)

    def token_grad():
        m = jnp.broadcast_to(jnp.sum(rowacc[...], axis=1, keepdims=True) / D, (TOK, 128))

        def one(i, _):
            f = ((i // 2) % 8 * 2 + i % 2) * 2 + i // 16
            cols = pl.ds(pl.multiple_of(f * 128, 128), 128)
            bb = back[:, pl.ds(pl.multiple_of(i * 128, 128), 128)]
            iv = inv_ref[...]
            sc = tok[:, cols].astype(F32) * iv
            tgo[:, cols] = (iv * (bb * gain[:, cols] - sc * m)).astype(BF16)
            return 0

        lax.fori_loop(0, 32, one, 0)
        stores.append(pltpu.make_async_copy(tgo, tg_h, st.at[2]))
        stores[-1].start()

    def start_second():
        ring_other(2)
        ring_own(3, yh)
        ring_other(3)
        to_sib(2, z)
        to_sib(3, z)

    def transposes():
        for r in range(3):
            arrived(ntr.at[r], nt_sem.at[r])

    def gain_core():
        push(go, gc, g_sem.at[0], sib)

    def gain_flip():
        arrived(gc, g_sem.at[0])
        g1[...] = go[...] + gc[...]
        push(g1, gy, g_sem.at[1], flip)

    def gain_ring():
        arrived(gy, g_sem.at[1])
        g2[...] = g1[...] + gy[...]
        for o in range(1, NZ):
            push(g2, gz.at[z], gz_sem.at[z], at(mod8(z + o), yh, c))
        gz[z] = g2[...]

    def gain_sum():
        for o in range(1, NZ):
            zz = mod8(z + o)
            arrived(gz.at[zz], gz_sem.at[zz])
        total = gz[0]
        for j in range(1, NZ):
            total += gz[j]
        gsum[...] = total
        stores.append(pltpu.make_async_copy(gsum, gg_h, st.at[4]))
        stores[-1].start()

    def weight_store():
        stores.append(pltpu.make_async_copy(wgo, wg_h, st.at[3]))
        stores[-1].start()

    def zero_rows():
        rowacc[...] = jnp.zeros_like(rowacc)

    plan = (
        (gather_step, 0, 1),
        (drift_out,),
        (gather_step, 0, 2),
        (start_second,),
        (gather_step, 0, 3),
        (loads[2].wait,),
        (gather_step, 0, 4),
        (project, 0),
        (gather_step, 1, 1),
        (drift_sum,),
        (back_first, 0, 8),
        (gather_step, 1, 2),
        (back_first, 8, 16),
        (pass_error, 0),
        (gather_step, 1, 3),
        (have_error, 0),
        (transposes,),
        (reduce_step, 0, 0),
        (outer_step,),
        (zero_rows,),
        (gather_step, 1, 4),
        (project, 1),
        (reduce_step, 0, 1),
        (back_rest, 0, 4),
        (pass_error, 1),
        (reduce_step, 0, 2),
        (have_error, 1),
        (reduce_step, 1, 0),
        (back_rest, 4, 10),
        (reduce_step, 0, 3),
        (reduce_step, 1, 1),
        (back_rest, 10, 16),
        (gain_core,),
        (reduce_step, 1, 2),
        (reduce_last, 0),
        (gain_flip,),
        (token_grad,),
        (reduce_step, 1, 3),
        (gain_ring,),
        (reduce_last, 1),
        (weight_store,),
        (gain_sum,),
    )
    for stage, *args in plan:
        stage(*args)
    for cp in sends:
        cp.wait_send()
    for cp in stores:
        cp.wait()


def hand_on(*refs):
    n = len(refs) // 3
    ins, outs, held, sems = refs[:n], refs[n:2 * n], refs[2 * n:3 * n], refs[3 * n]
    first = [pltpu.make_async_copy(ins[i], held[i], sems.at[0, i]) for i in range(n)]
    second = [pltpu.make_async_copy(held[i], outs[i], sems.at[1, i]) for i in range(n)]
    for cp in first:
        cp.start()
    for a, b in zip(first, second):
        a.wait()
        b.start()
    for cp in second:
        cp.wait()


def on_device(tokens, target, kv_weight, norm_gain, global_frag, momentum, local_frag):
    sem = pltpu.SemaphoreType.DMA
    vm = pltpu.VMEM
    anyspec = pl.BlockSpec(memory_space=pl.ANY)
    outs = (
        jax.ShapeDtypeStruct((128, 1024), BF16),
        jax.ShapeDtypeStruct((TOK, D), BF16),
        jax.ShapeDtypeStruct((32, 128), F32),
        jax.ShapeDtypeStruct((256, 1024), F32),
        jax.ShapeDtypeStruct((256, 1024), F32),
    )
    wg, tg, gg, ng, nm = pl.pallas_call(
        kernel,
        out_shape=outs,
        in_specs=[anyspec] * 7,
        out_specs=[anyspec] * 5,
        scratch_shapes=[
            vm((TOK, D), BF16),
            vm((TOK, 1024), BF16),
            vm((1, D), F32),
            vm((256, 1024), F32),
            vm((256, 1024), F32),
            vm((256, 1024), F32),
            vm((NQ, 2, NZ, 256, QC), BF16),
            vm((TOK, D), BF16),
            vm((2, 2, NZ, 128, TOK), BF16),
            vm((3, NZ, 128, TOK), BF16),
            vm((4, NQ, TOK, QC), BF16),
            vm((NQ, 2, 4, 128, QC), BF16),
            vm((NQ, 2, 4, 128, QC), BF16),
            vm((TOK, D), F32),
            vm((TOK, D), BF16),
            vm((128, 1024), BF16),
            vm((8, 32, 1024), BF16),
            vm((8, 32, 1024), BF16),
            vm((8, 32, 1024), BF16),
            vm((32, 128), F32),
            vm((32, 128), F32),
            vm((32, 128), F32),
            vm((32, 128), F32),
            vm((32, 128), F32),
            vm((NZ, 32, 128), F32),
            vm((32, 128), F32),
            vm((TOK, 128), F32),
            vm((TOK, 128), F32),
            sem((NQ + 6,)),
            sem((5,)),
            sem((NSEND,)),
            sem((NQ, 2, 4)),
            sem((NQ,)),
            sem((NQ,)),
            sem((3,)),
            sem((3, NQ)),
            sem((NQ, 2, 4)),
            sem((8,)),
            sem((8,)),
            sem((2,)),
            sem((NZ,)),
        ],
        compiler_params=pltpu.CompilerParams(
            collective_id=0, has_side_effects=True, vmem_limit_bytes=60 * 2**20),
        cost_estimate=pl.CostEstimate(flops=6 * 2**30, bytes_accessed=12 * 2**20, transcendentals=256),
        name="step",
    )(
        tokens, target, kv_weight[0], norm_gain,
        global_frag.reshape(256, 1024), momentum.reshape(256, 1024), local_frag.reshape(256, 1024),
    )
    wg, tg, gg, ng, nm = pl.pallas_call(
        hand_on,
        out_shape=outs,
        in_specs=[anyspec] * 5,
        out_specs=[anyspec] * 5,
        scratch_shapes=[vm(o.shape, o.dtype) for o in outs] + [sem((2, 5))],
        compiler_params=pltpu.CompilerParams(vmem_limit_bytes=56 * 2**20),
        name="hand_on",
    )(wg, tg, gg, ng, nm)
    return (wg[None], tg, gg.reshape(1, D), ng.reshape(2, 128, 1024), nm.reshape(2, 128, 1024))


def solution(mesh):
    placed = (
        P(("island", "fsdp"), None),
        P(("island", "fsdp"), None),
        P("island", "fsdp", None),
        P("island", None),
        P(None, "fsdp", None),
        P(None, "fsdp", None),
        P("island", None, "fsdp", None),
    )
    return jax.shard_map(
        on_device,
        mesh=mesh,
        in_specs=placed,
        out_specs=(
            P("island", "fsdp", None),
            P(("island", "fsdp"), None),
            P("island", None),
            P(None, "fsdp", None),
            P(None, "fsdp", None),
        ),
        check_vma=False,
    )
```

```python
import math

import jax
import jax.numpy as jnp
from jax import lax
from jax.experimental import pallas as pl
from jax.experimental.pallas import tpu as pltpu
from jax.sharding import PartitionSpec as P

MESH = pl.DeviceIdType.MESH
BF16 = jnp.bfloat16
F32 = jnp.float32
GROUPS = ((0, 1), (2, 3))
WIDTH = (256, 256, 256, 256)
START = (0, 256, 512, 768)
NB = len(WIDTH)
SPLIT = (9, 9)
NZ = 8
NX = 4
TOK = 256
D = 4096
PLUS, MINUS = 0, 1
NSEND = 256


def hops(q, way):
    return 4 if (q % 2) == way else 3


def nt_dot(a, b):
    return lax.dot_general(a, b, (((1,), (1,)), ((), ())), preferred_element_type=F32)


def kernel(*refs):
    refs = list(refs)

    def take(n):
        out = refs[:n]
        del refs[:n]
        return out

    tok_h, tgt_h, w_h, gain_h, glob_h, mom_h, loc_h = take(7)
    wg_h, tg_h, gg_h, ng_h, nm_h = take(5)
    tok, tgt, gain, glob, mom, loc, normed, nto, ntr, back, tgo, wgo = take(12)
    dr, dp, dq, osb, go, gc, g1, gy, g2, gz, gsum, rowacc, inv_ref = take(13)
    wb, errb, rss, rsr = take(NB), take(NB), take(NB), take(NB)
    ld, st, send, ag_sem, y_sem, mix_sem, sib_sem, nt_sem, err_sem, rs_sem, d_sem, p_sem, o_sem, g_sem, gz_sem = take(15)

    isl = lax.axis_index("island")
    fs = lax.axis_index("fsdp")
    z = fs // 4
    yh = (fs // 2) % 2
    c = fs % 2
    yl = isl // NX
    x = isl % NX

    def at(zz, yy, cc):
        return (isl, (zz * 2 + yy) * 2 + cc)

    def mod8(v):
        return lax.rem(v + 8, 8)

    def along_x(o):
        return lax.rem(x + o, NX)

    ring = (at(mod8(z + 1), yh, c), at(mod8(z - 1), yh, c))
    sib = at(z, yh, 1 - c)
    flip = at(z, 1 - yh, c)
    diag = at(z, 1 - yh, 1 - c)
    low = ((1 - yl) * NX + x, fs)

    sends = []
    stores = []

    def push(src, dst, sem, dev):
        cp = pltpu.make_async_remote_copy(
            src_ref=src, dst_ref=dst, send_sem=send.at[len(sends)], recv_sem=sem,
            device_id=dev, device_id_type=MESH)
        cp.start()
        sends.append(cp)

    def arrived(ref, sem):
        pltpu.make_async_copy(ref, ref, sem).wait()

    def store(src, dst):
        cp = pltpu.make_async_copy(src, dst, st.at[len(stores)])
        cp.start()
        stores.append(cp)

    loads_w = [pltpu.make_async_copy(
        w_h.at[:, pl.ds(START[q], WIDTH[q])], wb[q].at[c, z, pl.ds(yh * 128, 128)], ld.at[q]) for q in range(NB)]
    for cp in loads_w:
        cp.start()
    loads = [pltpu.make_async_copy(s, d, ld.at[NB + i]) for i, (s, d) in enumerate(
        ((tok_h, tok), (gain_h, gain), (tgt_h, tgt), (glob_h, glob), (loc_h, loc), (mom_h, mom)))]
    for cp in loads:
        cp.start()

    bar = pltpu.get_barrier_semaphore()
    partners = [at(mod8(z + o), yh, c) for o in range(1, NZ)] + [sib, flip, diag, low]
    partners += [(yl * NX + along_x(o), fs) for o in range(1, NX)]
    for dev in partners:
        pl.semaphore_signal(bar, inc=1, device_id=dev, device_id_type=MESH)
    pl.semaphore_wait(bar, len(partners))

    def piece(q, zz):
        return wb[q].at[c, zz]

    def half(q, zz, yy):
        return wb[q].at[c, zz, pl.ds(yy * 128, 128)]

    def ring_own(q, yy):
        for way in (PLUS, MINUS):
            push(half(q, z, yy), half(q, z, yy), ag_sem.at[q, way, 0], ring[way])

    def to_sib(q, zz):
        push(piece(q, zz), piece(q, zz), sib_sem.at[q], sib)

    def ring_other(q):
        arrived(half(q, z, 1 - yh), y_sem.at[q])
        ring_own(q, 1 - yh)

    for q in range(NB):
        loads_w[q].wait()
        push(half(q, z, yh), half(q, z, yh), y_sem.at[q], flip)
        if q < 2:
            ring_own(q, yh)

    loads[0].wait()

    def squares(i, acc):
        t = tok[:, pl.ds(pl.multiple_of(i * 128, 128), 128)].astype(F32)
        return acc + t * t

    acc = lax.fori_loop(0, 32, squares, jnp.zeros((TOK, 128), F32), unroll=4)
    inv_ref[...] = jnp.broadcast_to(
        lax.rsqrt(jnp.sum(acc, axis=1, keepdims=True) / D + 1e-05), (TOK, 128))

    for q in (0, 1):
        ring_other(q)
    for q in (2, 3):
        ring_own(q, yh)
    for q in (0, 1):
        to_sib(q, z)

    loads[1].wait()

    def norm_block(i, _):
        bc, bz, by = i // 16, (i // 2) % 8, i % 2
        f = (bz * 2 + by) * 2 + bc
        cols = pl.ds(pl.multiple_of(f * 128, 128), 128)
        n = (tok[:, cols].astype(F32) * inv_ref[...] * gain[:, cols]).astype(BF16)
        normed[:, pl.ds(pl.multiple_of(i * 128, 128), 128)] = n
        nto[by, bc, bz] = n.T
        return 0

    lax.fori_loop(0, 32, norm_block, 0, unroll=2)
    push(nto.at[yh, 1 - c], ntr.at[0], nt_sem.at[0], sib)

    def send_normed(lo, hi):
        for zz in range(lo, hi):
            push(nto.at[1 - yh, c, zz], ntr.at[1, zz], nt_sem.at[1], flip)
            push(nto.at[1 - yh, 1 - c, zz], ntr.at[2, zz], nt_sem.at[2], diag)

    def have_normed():
        for r in range(3):
            arrived(ntr.at[r], nt_sem.at[r])

    def ring_group(g):
        for q in GROUPS[g]:
            if g > 1:
                ring_own(q, yh)
            ring_other(q)
        for q in GROUPS[g]:
            to_sib(q, z)

    def gather_step(g, s):
        for q in GROUPS[g]:
            for way in (PLUS, MINUS):
                k = hops(q, way)
                if s > k:
                    continue
                zz = mod8(z - s) if way == PLUS else mod8(z + s)
                if s < SPLIT[g]:
                    arrived(piece(q, zz), ag_sem.at[q, way, s - 1])
                else:
                    arrived(half(q, zz, yh), ag_sem.at[q, way, s - 1])
                if s < k:
                    block = piece(q, zz) if s + 1 < SPLIT[g] else half(q, zz, yh)
                    push(block, block, ag_sem.at[q, way, s], ring[way])
                if s < SPLIT[g]:
                    to_sib(q, zz)
                else:
                    push(half(q, zz, yh), half(q, zz, yh), mix_sem.at[q, way, s - 3], flip)

    def mix(g):
        for s in range(SPLIT[g], 5):
            for q in GROUPS[g]:
                for way in (PLUS, MINUS):
                    if s <= hops(q, way):
                        zz = mod8(z - s) if way == PLUS else mod8(z + s)
                        arrived(half(q, zz, 1 - yh), mix_sem.at[q, way, s - 3])
                        to_sib(q, zz)

    def project(g):
        for q in GROUPS[g]:
            w = WIDTH[q]
            arrived(wb[q].at[1 - c], sib_sem.at[q])
            p = jnp.dot(normed[...], wb[q][...].reshape(D, w), preferred_element_type=F32)
            errb[q][0] = (p - tgt[:, START[q]:START[q] + w].astype(F32)).astype(BF16)
            push(errb[q].at[0], errb[q].at[2], err_sem.at[1, q], flip)
            push(errb[q].at[0], errb[q].at[1], err_sem.at[0, q], sib)

    def pass_error(g):
        for q in GROUPS[g]:
            arrived(errb[q].at[2], err_sem.at[1, q])
            push(errb[q].at[2], errb[q].at[3], err_sem.at[2, q], sib)

    def have_error(g):
        for q in GROUPS[g]:
            arrived(errb[q].at[1], err_sem.at[0, q])
            arrived(errb[q].at[3], err_sem.at[2, q])

    def term(q, zz):
        p = jnp.dot(nto[yh, c, zz], errb[q][0], preferred_element_type=F32)
        for r in range(3):
            p += jnp.dot(ntr[r, zz], errb[q][r + 1], preferred_element_type=F32)
        return p

    def reduce_step(g, s):
        for q in GROUPS[g]:
            for way in (PLUS, MINUS):
                k = hops(q, way)
                if s >= k:
                    continue
                p = term(q, mod8(z + (k - s)) if way == PLUS else mod8(z - (k - s)))
                if s > 0:
                    arrived(rsr[q].at[way, s - 1], rs_sem.at[q, way, s - 1])
                    p += rsr[q][way, s - 1].astype(F32)
                rss[q][way, s] = p.astype(BF16)
                push(rss[q].at[way, s], rsr[q].at[way, s], rs_sem.at[q, way, s], ring[way])

    loss_scale = 1.0 / math.sqrt(TOK * 32)

    def reduce_last(g):
        for q in GROUPS[g]:
            p = term(q, z)
            for way in (PLUS, MINUS):
                s = hops(q, way) - 1
                arrived(rsr[q].at[way, s], rs_sem.at[q, way, s])
                p += rsr[q][way, s].astype(F32)
            cols = slice(START[q], START[q] + WIDTH[q])
            wgo[:, cols] = (p * loss_scale).astype(BF16)
        first = START[GROUPS[g][0]]
        cols = pl.ds(first, 2 * WIDTH[GROUPS[g][0]])
        store(wgo.at[:, cols], wg_h.at[:, cols])

    def x_rows(j):
        return pl.ds(pl.multiple_of(j * 64, 64), 64)

    def drift_out():
        loads[3].wait()
        loads[4].wait()

        def one(j, _):
            loc[x_rows(j), :] = glob[x_rows(j), :] - loc[x_rows(j), :]
            return 0

        lax.fori_loop(0, NX, one, 0)
        for o in range(1, NX):
            j = along_x(o)
            push(loc.at[x_rows(j)], dr.at[x], d_sem.at[x], (yl * NX + j, fs))
        dr[x] = loc[x_rows(x), :]

    def drift_pair():
        for o in range(1, NX):
            arrived(dr.at[along_x(o)], d_sem.at[along_x(o)])
        dp[...] = (dr[0] + dr[1]) + (dr[2] + dr[3])
        push(dp, dq, p_sem.at[0], low)

    def drift_back():
        arrived(dq, p_sem.at[0])
        osb[x] = (dp[...] + dq[...]) / 8
        for o in range(1, NX):
            push(osb.at[x], osb.at[x], o_sem.at[x], (yl * NX + along_x(o), fs))

    def outer_step():
        loads[5].wait()
        for o in range(1, NX):
            arrived(osb.at[along_x(o)], o_sem.at[along_x(o)])

        def one(j, _):
            rows = pl.ds(pl.multiple_of(j * 64, 64), 64)
            outer = osb[j]
            nm = 0.9 * mom[rows, :] + outer
            mom[rows, :] = nm
            glob[rows, :] = glob[rows, :] - 0.7 * (outer + 0.9 * nm)
            return 0

        lax.fori_loop(0, NX, one, 0)
        store(mom, nm_h)
        store(glob, ng_h)

    def back_part(g, lo, hi):
        def one(kb, _):
            bc, bz = kb // 8, kb % 8
            here = pl.ds(pl.multiple_of(kb * 256, 256), 256)
            b = nt_dot(errb[GROUPS[g][0]][0], wb[GROUPS[g][0]][bc, bz])
            b += nt_dot(errb[GROUPS[g][1]][0], wb[GROUPS[g][1]][bc, bz])
            back[:, here] = b if g == 0 else back[:, here] + b
            return 0

        lax.fori_loop(lo, hi, one, 0)

    def back_rest(lo, hi):
        def one(kb, _):
            bc, bz = kb // 8, kb % 8
            here = pl.ds(pl.multiple_of(kb * 256, 256), 256)
            b = back[:, here]
            for q in GROUPS[1]:
                b += nt_dot(errb[q][0], wb[q][bc, bz])
            back[:, here] = b
            for by in range(2):
                f = (bz * 2 + by) * 2 + bc
                cols = pl.ds(pl.multiple_of(f * 128, 128), 128)
                bs = b[:, by * 128:(by + 1) * 128] * (tok[:, cols].astype(F32) * inv_ref[...])
                go[pl.ds(f, 1), :] = jnp.sum(bs, axis=0, keepdims=True)
                rowacc[...] += bs * gain[:, cols]
            return 0

        lax.fori_loop(lo, hi, one, 0)

    def token_grad():
        m = jnp.broadcast_to(jnp.sum(rowacc[...], axis=1, keepdims=True) / D, (TOK, 128))

        def one(i, _):
            f = ((i // 2) % 8 * 2 + i % 2) * 2 + i // 16
            cols = pl.ds(pl.multiple_of(f * 128, 128), 128)
            bb = back[:, pl.ds(pl.multiple_of(i * 128, 128), 128)]
            iv = inv_ref[...]
            sc = tok[:, cols].astype(F32) * iv
            tgo[:, cols] = (iv * (bb * gain[:, cols] - sc * m)).astype(BF16)
            return 0

        lax.fori_loop(0, 32, one, 0)
        store(tgo, tg_h)

    def gain_core():
        push(go, gc, g_sem.at[0], sib)

    def gain_flip():
        arrived(gc, g_sem.at[0])
        g1[...] = go[...] + gc[...]
        push(g1, gy, g_sem.at[1], flip)

    def gain_ring():
        arrived(gy, g_sem.at[1])
        g2[...] = g1[...] + gy[...]
        for o in range(1, NZ):
            push(g2, gz.at[z], gz_sem.at[z], at(mod8(z + o), yh, c))
        gz[z] = g2[...]

    def gain_sum():
        for o in range(1, NZ):
            zz = mod8(z + o)
            arrived(gz.at[zz], gz_sem.at[zz])
        total = gz[0]
        for j in range(1, NZ):
            total += gz[j]
        gsum[...] = total
        store(gsum, gg_h)

    done = [0, 0]

    def settle():
        for cp in sends[done[0]:done[1]]:
            cp.wait_send()
        done[:] = [done[1], len(sends)]

    def zero_rows():
        rowacc[...] = jnp.zeros_like(rowacc)

    plan = (
        (gather_step, 0, 1),
        (drift_out,),
        (send_normed, 0, 8),
        (gather_step, 0, 2),
        (ring_group, 1),
        (gather_step, 0, 3),
        (settle,),
        (loads[2].wait,),
        (gather_step, 1, 1),
        (gather_step, 0, 4),
        (project, 0),
        (zero_rows,),
        (gather_step, 1, 2),
        (drift_pair,),
        (back_part, 0, 0, 16),
        (settle,),
        (gather_step, 1, 3),
        (pass_error, 0),
        (have_error, 0),
        (have_normed,),
        (reduce_step, 0, 0),
        (settle,),
        (gather_step, 1, 4),
        (project, 1),
        (drift_back,),
        (reduce_step, 0, 1),
        (pass_error, 1),
        (back_rest, 0, 3),
        (reduce_step, 0, 2),
        (have_error, 1),
        (reduce_step, 1, 0),
        (settle,),
        (back_rest, 3, 8),
        (reduce_step, 0, 3),
        (reduce_step, 1, 1),
        (back_rest, 8, 16),
        (gain_core,),
        (reduce_step, 1, 2),
        (reduce_last, 0),
        (gain_flip,),
        (settle,),
        (token_grad,),
        (reduce_step, 1, 3),
        (outer_step,),
        (gain_ring,),
        (settle,),
        (reduce_last, 1),
        (gain_sum,),
    )
    for stage, *args in plan:
        stage(*args)
    for cp in sends[done[0]:]:
        cp.wait_send()
    for cp in stores:
        cp.wait()


def hand_on(*refs):
    n = len(refs) // 3
    ins, outs, held, sems = refs[:n], refs[n:2 * n], refs[2 * n:3 * n], refs[3 * n]
    first = [pltpu.make_async_copy(ins[i], held[i], sems.at[0, i]) for i in range(n)]
    second = [pltpu.make_async_copy(held[i], outs[i], sems.at[1, i]) for i in range(n)]
    for cp in first:
        cp.start()
    for a, b in zip(first, second):
        a.wait()
        b.start()
    for cp in second:
        cp.wait()


def on_device(tokens, target, kv_weight, norm_gain, global_frag, momentum, local_frag):
    sem = pltpu.SemaphoreType.DMA
    vm = pltpu.VMEM
    anyspec = pl.BlockSpec(memory_space=pl.ANY)
    outs = (
        jax.ShapeDtypeStruct((128, 1024), BF16),
        jax.ShapeDtypeStruct((TOK, D), BF16),
        jax.ShapeDtypeStruct((32, 128), F32),
        jax.ShapeDtypeStruct((256, 1024), F32),
        jax.ShapeDtypeStruct((256, 1024), F32),
    )
    wg, tg, gg, ng, nm = pl.pallas_call(
        kernel,
        out_shape=outs,
        in_specs=[anyspec] * 7,
        out_specs=[anyspec] * 5,
        scratch_shapes=[
            vm((TOK, D), BF16),
            vm((TOK, 1024), BF16),
            vm((1, D), F32),
            vm((256, 1024), F32),
            vm((256, 1024), F32),
            vm((256, 1024), F32),
            vm((TOK, D), BF16),
            vm((2, 2, NZ, 128, TOK), BF16),
            vm((3, NZ, 128, TOK), BF16),
            vm((TOK, D), F32),
            vm((TOK, D), BF16),
            vm((128, 1024), BF16),
            vm((NX, 64, 1024), F32),
            vm((64, 1024), F32),
            vm((64, 1024), F32),
            vm((NX, 64, 1024), F32),
            vm((32, 128), F32),
            vm((32, 128), F32),
            vm((32, 128), F32),
            vm((32, 128), F32),
            vm((32, 128), F32),
            vm((NZ, 32, 128), F32),
            vm((32, 128), F32),
            vm((TOK, 128), F32),
            vm((TOK, 128), F32),
        ]
        + [vm((2, NZ, 256, w), BF16) for w in WIDTH]
        + [vm((4, TOK, w), BF16) for w in WIDTH]
        + [vm((2, 4, 128, w), BF16) for w in WIDTH]
        + [vm((2, 4, 128, w), BF16) for w in WIDTH]
        + [
            sem((NB + 6,)),
            sem((8,)),
            sem((NSEND,)),
            sem((NB, 2, 4)),
            sem((NB,)),
            sem((NB, 2, 2)),
            sem((NB,)),
            sem((3,)),
            sem((3, NB)),
            sem((NB, 2, 4)),
            sem((NX,)),
            sem((1,)),
            sem((NX,)),
            sem((2,)),
            sem((NZ,)),
        ],
        compiler_params=pltpu.CompilerParams(
            collective_id=0, has_side_effects=True, vmem_limit_bytes=60 * 2**20),
        cost_estimate=pl.CostEstimate(flops=6 * 2**30, bytes_accessed=12 * 2**20, transcendentals=256),
        name="step",
    )(
        tokens, target, kv_weight[0], norm_gain,
        global_frag.reshape(256, 1024), momentum.reshape(256, 1024), local_frag.reshape(256, 1024),
    )
    wg, tg, gg, ng, nm = pl.pallas_call(
        hand_on,
        out_shape=outs,
        in_specs=[anyspec] * 5,
        out_specs=[anyspec] * 5,
        scratch_shapes=[vm(o.shape, o.dtype) for o in outs] + [sem((2, 5))],
        compiler_params=pltpu.CompilerParams(vmem_limit_bytes=56 * 2**20),
        name="hand_on",
    )(wg, tg, gg, ng, nm)
    return (wg[None], tg, gg.reshape(1, D), ng.reshape(2, 128, 1024), nm.reshape(2, 128, 1024))


def solution(mesh):
    placed = (
        P(("island", "fsdp"), None),
        P(("island", "fsdp"), None),
        P("island", "fsdp", None),
        P("island", None),
        P(None, "fsdp", None),
        P(None, "fsdp", None),
        P("island", None, "fsdp", None),
    )
    return jax.shard_map(
        on_device,
        mesh=mesh,
        in_specs=placed,
        out_specs=(
            P("island", "fsdp", None),
            P(("island", "fsdp"), None),
            P("island", None),
            P(None, "fsdp", None),
            P(None, "fsdp", None),
        ),
        check_vma=False,
    )
```

```python
import math

import jax
import jax.numpy as jnp
from jax import lax
from jax.experimental import pallas as pl
from jax.experimental.pallas import tpu as pltpu
from jax.sharding import PartitionSpec as P

MESH = pl.DeviceIdType.MESH
BF16 = jnp.bfloat16
F32 = jnp.float32
GROUPS = ((0, 1), (2, 3))
WIDTH = (256, 256, 256, 256)
START = (0, 256, 512, 768)
NB = len(WIDTH)
SPLIT = (9, 9)
NZ = 8
NX = 4
TOK = 256
D = 4096
PLUS, MINUS = 0, 1
NSEND = 256


def hops(q, way):
    return 4 if (q % 2) == way else 3


def nt_dot(a, b):
    return lax.dot_general(a, b, (((1,), (1,)), ((), ())), preferred_element_type=F32)


def kernel(*refs):
    refs = list(refs)

    def take(n):
        out = refs[:n]
        del refs[:n]
        return out

    tok_h, tgt_h, w_h, gain_h, glob_h, mom_h, loc_h = take(7)
    wg_h, tg_h, gg_h, ng_h, nm_h = take(5)
    tok, tgt, gain, glob, mom, loc, normed, nto, ntr, back, tgo, wgo = take(12)
    dr, dp, dq, osb, go, gc, g1, gy, g2, gz, gsum, rowacc, inv_ref = take(13)
    wb, errb, rss, rsr = take(NB), take(NB), take(NB), take(NB)
    ld, st, send, ag_sem, y_sem, mix_sem, sib_sem, nt_sem, err_sem, rs_sem, d_sem, p_sem, o_sem, g_sem, gz_sem = take(15)

    isl = lax.axis_index("island")
    fs = lax.axis_index("fsdp")
    z = fs // 4
    yh = (fs // 2) % 2
    c = fs % 2
    yl = isl // NX
    x = isl % NX

    def at(zz, yy, cc):
        return (isl, (zz * 2 + yy) * 2 + cc)

    def mod8(v):
        return lax.rem(v + 8, 8)

    def along_x(o):
        return lax.rem(x + o, NX)

    ring = (at(mod8(z + 1), yh, c), at(mod8(z - 1), yh, c))
    sib = at(z, yh, 1 - c)
    flip = at(z, 1 - yh, c)
    diag = at(z, 1 - yh, 1 - c)
    low = ((1 - yl) * NX + x, fs)

    sends = []
    stores = []

    def push(src, dst, sem, dev):
        cp = pltpu.make_async_remote_copy(
            src_ref=src, dst_ref=dst, send_sem=send.at[len(sends)], recv_sem=sem,
            device_id=dev, device_id_type=MESH)
        cp.start()
        sends.append(cp)

    def arrived(ref, sem):
        pltpu.make_async_copy(ref, ref, sem).wait()

    def store(src, dst):
        cp = pltpu.make_async_copy(src, dst, st.at[len(stores)])
        cp.start()
        stores.append(cp)

    loads_w = [pltpu.make_async_copy(
        w_h.at[:, pl.ds(START[q], WIDTH[q])], wb[q].at[c, z, pl.ds(yh * 128, 128)], ld.at[q]) for q in range(NB)]
    for cp in loads_w:
        cp.start()
    loads = [pltpu.make_async_copy(s, d, ld.at[NB + i]) for i, (s, d) in enumerate(
        ((tok_h, tok), (gain_h, gain), (tgt_h, tgt), (glob_h, glob), (loc_h, loc), (mom_h, mom)))]
    for cp in loads:
        cp.start()

    bar = pltpu.get_barrier_semaphore()
    partners = [at(mod8(z + o), yh, c) for o in range(1, NZ)] + [sib, flip, diag, low]
    partners += [(yl * NX + along_x(o), fs) for o in range(1, NX)]
    for dev in partners:
        pl.semaphore_signal(bar, inc=1, device_id=dev, device_id_type=MESH)
    pl.semaphore_wait(bar, len(partners))

    def piece(q, zz):
        return wb[q].at[c, zz]

    def half(q, zz, yy):
        return wb[q].at[c, zz, pl.ds(yy * 128, 128)]

    def ring_own(q, yy):
        for way in (PLUS, MINUS):
            push(half(q, z, yy), half(q, z, yy), ag_sem.at[q, way, 0], ring[way])

    def to_sib(q, zz):
        push(piece(q, zz), piece(q, zz), sib_sem.at[q], sib)

    def ring_other(q):
        arrived(half(q, z, 1 - yh), y_sem.at[q])
        ring_own(q, 1 - yh)

    for q in range(NB):
        loads_w[q].wait()
        push(half(q, z, yh), half(q, z, yh), y_sem.at[q], flip)
        if q < 2:
            ring_own(q, yh)

    loads[0].wait()

    def squares(i, acc):
        t = tok[:, pl.ds(pl.multiple_of(i * 128, 128), 128)].astype(F32)
        return acc + t * t

    acc = lax.fori_loop(0, 32, squares, jnp.zeros((TOK, 128), F32), unroll=4)
    inv_ref[...] = jnp.broadcast_to(
        lax.rsqrt(jnp.sum(acc, axis=1, keepdims=True) / D + 1e-05), (TOK, 128))

    for q in (0, 1):
        ring_other(q)
    for q in (2, 3):
        ring_own(q, yh)
    for q in (0, 1):
        to_sib(q, z)

    loads[1].wait()

    def norm_block(i, _):
        bc, bz, by = i // 16, (i // 2) % 8, i % 2
        f = (bz * 2 + by) * 2 + bc
        cols = pl.ds(pl.multiple_of(f * 128, 128), 128)
        n = (tok[:, cols].astype(F32) * inv_ref[...] * gain[:, cols]).astype(BF16)
        normed[:, pl.ds(pl.multiple_of(i * 128, 128), 128)] = n
        nto[by, bc, bz] = n.T
        return 0

    lax.fori_loop(0, 32, norm_block, 0, unroll=2)
    push(nto.at[yh, 1 - c], ntr.at[0], nt_sem.at[0], sib)

    def send_normed(lo, hi):
        for zz in range(lo, hi):
            push(nto.at[1 - yh, c, zz], ntr.at[1, zz], nt_sem.at[1], flip)
            push(nto.at[1 - yh, 1 - c, zz], ntr.at[2, zz], nt_sem.at[2], diag)

    def have_normed():
        for r in range(3):
            arrived(ntr.at[r], nt_sem.at[r])

    def ring_group(g):
        for q in GROUPS[g]:
            if g > 1:
                ring_own(q, yh)
            ring_other(q)
        for q in GROUPS[g]:
            to_sib(q, z)

    def gather_step(g, s):
        for q in GROUPS[g]:
            for way in (PLUS, MINUS):
                k = hops(q, way)
                if s > k:
                    continue
                zz = mod8(z - s) if way == PLUS else mod8(z + s)
                if s < SPLIT[g]:
                    arrived(piece(q, zz), ag_sem.at[q, way, s - 1])
                else:
                    arrived(half(q, zz, yh), ag_sem.at[q, way, s - 1])
                if s < k:
                    block = piece(q, zz) if s + 1 < SPLIT[g] else half(q, zz, yh)
                    push(block, block, ag_sem.at[q, way, s], ring[way])
                if s < SPLIT[g]:
                    to_sib(q, zz)
                else:
                    push(half(q, zz, yh), half(q, zz, yh), mix_sem.at[q, way, s - 3], flip)

    def mix(g):
        for s in range(SPLIT[g], 5):
            for q in GROUPS[g]:
                for way in (PLUS, MINUS):
                    if s <= hops(q, way):
                        zz = mod8(z - s) if way == PLUS else mod8(z + s)
                        arrived(half(q, zz, 1 - yh), mix_sem.at[q, way, s - 3])
                        to_sib(q, zz)

    def project(g):
        for q in GROUPS[g]:
            w = WIDTH[q]
            arrived(wb[q].at[1 - c], sib_sem.at[q])
            p = jnp.dot(normed[...], wb[q][...].reshape(D, w), preferred_element_type=F32)
            errb[q][0] = (p - tgt[:, START[q]:START[q] + w].astype(F32)).astype(BF16)
            push(errb[q].at[0], errb[q].at[2], err_sem.at[1, q], flip)
            push(errb[q].at[0], errb[q].at[1], err_sem.at[0, q], sib)

    def pass_error(g):
        for q in GROUPS[g]:
            arrived(errb[q].at[2], err_sem.at[1, q])
            push(errb[q].at[2], errb[q].at[3], err_sem.at[2, q], sib)

    def have_error(g):
        for q in GROUPS[g]:
            arrived(errb[q].at[1], err_sem.at[0, q])
            arrived(errb[q].at[3], err_sem.at[2, q])

    def term(q, zz):
        p = jnp.dot(nto[yh, c, zz], errb[q][0], preferred_element_type=F32)
        for r in range(3):
            p += jnp.dot(ntr[r, zz], errb[q][r + 1], preferred_element_type=F32)
        return p

    def reduce_step(g, s):
        for q in GROUPS[g]:
            for way in (PLUS, MINUS):
                k = hops(q, way)
                if s >= k:
                    continue
                p = term(q, mod8(z + (k - s)) if way == PLUS else mod8(z - (k - s)))
                if s > 0:
                    arrived(rsr[q].at[way, s - 1], rs_sem.at[q, way, s - 1])
                    p += rsr[q][way, s - 1].astype(F32)
                rss[q][way, s] = p.astype(BF16)
                push(rss[q].at[way, s], rsr[q].at[way, s], rs_sem.at[q, way, s], ring[way])

    loss_scale = 1.0 / math.sqrt(TOK * 32)

    def reduce_last(g):
        for q in GROUPS[g]:
            p = term(q, z)
            for way in (PLUS, MINUS):
                s = hops(q, way) - 1
                arrived(rsr[q].at[way, s], rs_sem.at[q, way, s])
                p += rsr[q][way, s].astype(F32)
            cols = slice(START[q], START[q] + WIDTH[q])
            wgo[:, cols] = (p * loss_scale).astype(BF16)
        first = START[GROUPS[g][0]]
        cols = pl.ds(first, 2 * WIDTH[GROUPS[g][0]])
        store(wgo.at[:, cols], wg_h.at[:, cols])

    def x_rows(j):
        return pl.ds(pl.multiple_of(j * 64, 64), 64)

    def drift_out():
        loads[3].wait()
        loads[4].wait()

        def one(j, _):
            loc[x_rows(j), :] = glob[x_rows(j), :] - loc[x_rows(j), :]
            return 0

        lax.fori_loop(0, NX, one, 0)
        for o in range(1, NX):
            j = along_x(o)
            push(loc.at[x_rows(j)], dr.at[x], d_sem.at[x], (yl * NX + j, fs))
        dr[x] = loc[x_rows(x), :]

    def drift_pair():
        for o in range(1, NX):
            arrived(dr.at[along_x(o)], d_sem.at[along_x(o)])
        dp[...] = (dr[0] + dr[1]) + (dr[2] + dr[3])
        push(dp, dq, p_sem.at[0], low)

    def drift_back():
        arrived(dq, p_sem.at[0])
        osb[x] = (dp[...] + dq[...]) / 8
        for o in range(1, NX):
            push(osb.at[x], osb.at[x], o_sem.at[x], (yl * NX + along_x(o), fs))

    def outer_step():
        loads[5].wait()
        for o in range(1, NX):
            arrived(osb.at[along_x(o)], o_sem.at[along_x(o)])

        def one(j, _):
            rows = pl.ds(pl.multiple_of(j * 64, 64), 64)
            outer = osb[j]
            nm = 0.9 * mom[rows, :] + outer
            mom[rows, :] = nm
            glob[rows, :] = glob[rows, :] - 0.7 * (outer + 0.9 * nm)
            return 0

        lax.fori_loop(0, NX, one, 0)
        store(mom, nm_h)
        store(glob, ng_h)

    def back_part(g, lo, hi):
        def one(kb, _):
            bc, bz = kb // 8, kb % 8
            here = pl.ds(pl.multiple_of(kb * 256, 256), 256)
            b = nt_dot(errb[GROUPS[g][0]][0], wb[GROUPS[g][0]][bc, bz])
            b += nt_dot(errb[GROUPS[g][1]][0], wb[GROUPS[g][1]][bc, bz])
            back[:, here] = b if g == 0 else back[:, here] + b
            return 0

        lax.fori_loop(lo, hi, one, 0)

    def back_rest(lo, hi):
        def one(kb, _):
            bc, bz = kb // 8, kb % 8
            here = pl.ds(pl.multiple_of(kb * 256, 256), 256)
            b = back[:, here]
            for q in GROUPS[1]:
                b += nt_dot(errb[q][0], wb[q][bc, bz])
            back[:, here] = b
            for by in range(2):
                f = (bz * 2 + by) * 2 + bc
                cols = pl.ds(pl.multiple_of(f * 128, 128), 128)
                bs = b[:, by * 128:(by + 1) * 128] * (tok[:, cols].astype(F32) * inv_ref[...])
                go[pl.ds(f, 1), :] = jnp.sum(bs, axis=0, keepdims=True)
                rowacc[...] += bs * gain[:, cols]
            return 0

        lax.fori_loop(lo, hi, one, 0)

    def token_grad():
        m = jnp.broadcast_to(jnp.sum(rowacc[...], axis=1, keepdims=True) / D, (TOK, 128))

        def one(i, _):
            f = ((i // 2) % 8 * 2 + i % 2) * 2 + i // 16
            cols = pl.ds(pl.multiple_of(f * 128, 128), 128)
            bb = back[:, pl.ds(pl.multiple_of(i * 128, 128), 128)]
            iv = inv_ref[...]
            sc = tok[:, cols].astype(F32) * iv
            tgo[:, cols] = (iv * (bb * gain[:, cols] - sc * m)).astype(BF16)
            return 0

        lax.fori_loop(0, 32, one, 0)
        store(tgo, tg_h)

    def gain_core():
        push(go, gc, g_sem.at[0], sib)

    def gain_flip():
        arrived(gc, g_sem.at[0])
        g1[...] = go[...] + gc[...]
        push(g1, gy, g_sem.at[1], flip)

    def gain_ring():
        arrived(gy, g_sem.at[1])
        g2[...] = g1[...] + gy[...]
        for o in range(1, NZ):
            push(g2, gz.at[z], gz_sem.at[z], at(mod8(z + o), yh, c))
        gz[z] = g2[...]

    def gain_sum():
        for o in range(1, NZ):
            zz = mod8(z + o)
            arrived(gz.at[zz], gz_sem.at[zz])
        total = gz[0]
        for j in range(1, NZ):
            total += gz[j]
        gsum[...] = total
        store(gsum, gg_h)

    done = [0, 0]

    def settle():
        for cp in sends[done[0]:done[1]]:
            cp.wait_send()
        done[:] = [done[1], len(sends)]

    def zero_rows():
        rowacc[...] = jnp.zeros_like(rowacc)

    plan = (
        (gather_step, 0, 1),
        (drift_out,),
        (send_normed, 0, 8),
        (gather_step, 0, 2),
        (ring_group, 1),
        (gather_step, 0, 3),
        (settle,),
        (loads[2].wait,),
        (gather_step, 1, 1),
        (gather_step, 0, 4),
        (project, 0),
        (zero_rows,),
        (gather_step, 1, 2),
        (drift_pair,),
        (back_part, 0, 0, 16),
        (settle,),
        (gather_step, 1, 3),
        (pass_error, 0),
        (have_error, 0),
        (have_normed,),
        (reduce_step, 0, 0),
        (settle,),
        (gather_step, 1, 4),
        (project, 1),
        (drift_back,),
        (reduce_step, 0, 1),
        (back_rest, 0, 3),
        (reduce_step, 0, 2),
        (pass_error, 1),
        (have_error, 1),
        (reduce_step, 1, 0),
        (settle,),
        (back_rest, 3, 8),
        (reduce_step, 0, 3),
        (reduce_step, 1, 1),
        (back_rest, 8, 16),
        (gain_core,),
        (reduce_step, 1, 2),
        (reduce_last, 0),
        (gain_flip,),
        (settle,),
        (token_grad,),
        (reduce_step, 1, 3),
        (outer_step,),
        (gain_ring,),
        (settle,),
        (reduce_last, 1),
        (gain_sum,),
    )
    for stage, *args in plan:
        stage(*args)
    for cp in sends[done[0]:]:
        cp.wait_send()
    for cp in stores:
        cp.wait()


def hand_on(*refs):
    n = len(refs) // 3
    ins, outs, held, sems = refs[:n], refs[n:2 * n], refs[2 * n:3 * n], refs[3 * n]
    first = [pltpu.make_async_copy(ins[i], held[i], sems.at[0, i]) for i in range(n)]
    second = [pltpu.make_async_copy(held[i], outs[i], sems.at[1, i]) for i in range(n)]
    for cp in first:
        cp.start()
    for a, b in zip(first, second):
        a.wait()
        b.start()
    for cp in second:
        cp.wait()


def on_device(tokens, target, kv_weight, norm_gain, global_frag, momentum, local_frag):
    sem = pltpu.SemaphoreType.DMA
    vm = pltpu.VMEM
    anyspec = pl.BlockSpec(memory_space=pl.ANY)
    outs = (
        jax.ShapeDtypeStruct((128, 1024), BF16),
        jax.ShapeDtypeStruct((TOK, D), BF16),
        jax.ShapeDtypeStruct((32, 128), F32),
        jax.ShapeDtypeStruct((256, 1024), F32),
        jax.ShapeDtypeStruct((256, 1024), F32),
    )
    wg, tg, gg, ng, nm = pl.pallas_call(
        kernel,
        out_shape=outs,
        in_specs=[anyspec] * 7,
        out_specs=[anyspec] * 5,
        scratch_shapes=[
            vm((TOK, D), BF16),
            vm((TOK, 1024), BF16),
            vm((1, D), F32),
            vm((256, 1024), F32),
            vm((256, 1024), F32),
            vm((256, 1024), F32),
            vm((TOK, D), BF16),
            vm((2, 2, NZ, 128, TOK), BF16),
            vm((3, NZ, 128, TOK), BF16),
            vm((TOK, D), F32),
            vm((TOK, D), BF16),
            vm((128, 1024), BF16),
            vm((NX, 64, 1024), F32),
            vm((64, 1024), F32),
            vm((64, 1024), F32),
            vm((NX, 64, 1024), F32),
            vm((32, 128), F32),
            vm((32, 128), F32),
            vm((32, 128), F32),
            vm((32, 128), F32),
            vm((32, 128), F32),
            vm((NZ, 32, 128), F32),
            vm((32, 128), F32),
            vm((TOK, 128), F32),
            vm((TOK, 128), F32),
        ]
        + [vm((2, NZ, 256, w), BF16) for w in WIDTH]
        + [vm((4, TOK, w), BF16) for w in WIDTH]
        + [vm((2, 4, 128, w), BF16) for w in WIDTH]
        + [vm((2, 4, 128, w), BF16) for w in WIDTH]
        + [
            sem((NB + 6,)),
            sem((8,)),
            sem((NSEND,)),
            sem((NB, 2, 4)),
            sem((NB,)),
            sem((NB, 2, 2)),
            sem((NB,)),
            sem((3,)),
            sem((3, NB)),
            sem((NB, 2, 4)),
            sem((NX,)),
            sem((1,)),
            sem((NX,)),
            sem((2,)),
            sem((NZ,)),
        ],
        compiler_params=pltpu.CompilerParams(
            collective_id=0, has_side_effects=True, vmem_limit_bytes=60 * 2**20),
        cost_estimate=pl.CostEstimate(flops=6 * 2**30, bytes_accessed=12 * 2**20, transcendentals=256),
        name="step",
    )(
        tokens, target, kv_weight[0], norm_gain,
        global_frag.reshape(256, 1024), momentum.reshape(256, 1024), local_frag.reshape(256, 1024),
    )
    wg, tg, gg, ng, nm = pl.pallas_call(
        hand_on,
        out_shape=outs,
        in_specs=[anyspec] * 5,
        out_specs=[anyspec] * 5,
        scratch_shapes=[vm(o.shape, o.dtype) for o in outs] + [sem((2, 5))],
        compiler_params=pltpu.CompilerParams(vmem_limit_bytes=56 * 2**20),
        name="hand_on",
    )(wg, tg, gg, ng, nm)
    return (wg[None], tg, gg.reshape(1, D), ng.reshape(2, 128, 1024), nm.reshape(2, 128, 1024))


def solution(mesh):
    placed = (
        P(("island", "fsdp"), None),
        P(("island", "fsdp"), None),
        P("island", "fsdp", None),
        P("island", None),
        P(None, "fsdp", None),
        P(None, "fsdp", None),
        P("island", None, "fsdp", None),
    )
    return jax.shard_map(
        on_device,
        mesh=mesh,
        in_specs=placed,
        out_specs=(
            P("island", "fsdp", None),
            P(("island", "fsdp"), None),
            P("island", None),
            P(None, "fsdp", None),
            P(None, "fsdp", None),
        ),
        check_vma=False,
    )
```
